512 devices in a mesh: tok: 16 (over z), col: 32 (over x, y, core).
Axes of the slice: x: 4, y: 4, z: 16, core: 2. Of those that a mesh axis runs over, the one named last changes fastest.
Arguments:
- acts: bfloat16 [8192, 28672], P('tok', 'col'), may hold values from -6 to 6
- residual: float32 [8192, 8192], P('tok', 'col'), may hold values from -6 to 6
- weights: bfloat16 [32, 896, 8192], P(None, 'tok', 'col'), may hold values from -6 to 6
- order: int32 [4], replicated, may hold values from 0 to 31
- rate: float32 [32], replicated, may hold values from 0.1 to 0.4
- penalty: float32 [32], replicated, may hold values from 0.4 to 1.2
Outputs:
- pruned: float32 [32, 896, 8192], P(None, 'tok', 'col')
- resid_out: float32 [8192, 8192], P('tok', 'col')
The draws below stay inside these ranges and needn't reach their ends.
Inputs may be any that keep to these rules, and one draw needn't show every extreme that they name: `order`: block indices, repeats allowed.
All inputs are finite; a program needn't handle non-finite values.
Results may differ from the reference program's by a relative error of at most 0.0054.
Values may be sent and summed in bfloat16 or wider, within the bound.
A program may use at most 64 MiB of HBM per device.

```python
import math
import jax
import jax.numpy as jnp
from jax import lax

D = 8192
CH = 28672
STEPS = 4
NBLK = 32
BLOCK = 896
TOKENS = 8192


def draw_weights(key, part):
    key = jax.random.fold_in(key, 11)
    scale_key, base_key = jax.random.split(key)
    row_scale = jnp.exp(jax.random.uniform(scale_key, (NBLK, BLOCK, 1), jnp.float32, jnp.log(0.05), jnp.log(1.0)))
    base = jnp.clip(jax.random.normal(base_key, (NBLK, BLOCK, D), jnp.float32), -6.0, 6.0)
    return (base * row_scale).astype(jnp.bfloat16)


def draw_residual(key, part):
    key = jax.random.fold_in(key, 13)
    level_key, base_key = jax.random.split(key)
    level = jnp.exp(jax.random.uniform(level_key, (32,), jnp.float32, -1.5, 1.5))
    column_level = jnp.repeat(level, D // 32)[None, :]
    base = jnp.clip(jax.random.normal(base_key, (TOKENS, D), jnp.float32), -6.0, 6.0)
    return jnp.clip(base * column_level, -6.0, 6.0)


def with_ends(values, stream_key, low, top_value):
    dims = values.shape
    index_at = [jax.random.randint(jax.random.fold_in(stream_key, axis), (), 0, dims[axis]) for axis in range(len(dims))]
    values = values.at[tuple(index_at)].set(low)
    longest = dims.index(max(dims))
    index_at[longest] = (index_at[longest] + 1) % dims[longest]
    return values.at[tuple(index_at)].set(top_value)


def shard_levels(own_key, dims, pieces, least, high):
    loudness, own = 1.0, jax.random.fold_in(own_key, 6)
    for axis_at, parts in pieces:
        heights = jnp.exp(jax.random.uniform(jax.random.fold_in(own, axis_at), (parts,), jnp.float32, least / len(pieces), high / len(pieces)))
        loudness = loudness * jnp.repeat(heights, dims[axis_at] // parts).reshape([-1 if axis == axis_at else 1 for axis in range(len(dims))])
    return loudness


def noise(key, shape, deviation, bound, pieces=(), held_as=jnp.bfloat16):
    factor_of = shard_levels(key, shape, pieces, -0.22, 0.18) if pieces else 1.0
    drawn = jax.random.normal(key, shape, jnp.float32) * deviation * factor_of
    return jnp.minimum(jnp.maximum(drawn, -bound), bound).astype(held_as)


def setup_inputs(seed: int = 0) -> dict:
    splits = jax.random.split(jax.random.key(seed), 7)
    return {
        "acts": noise(splits[0], (TOKENS, CH), 1.0, 6.0, ((0, 16), (1, 32))),
        "residual": draw_residual(jax.random.fold_in(splits[6], 71), 0),
        "weights": draw_weights(jax.random.fold_in(splits[6], 71), 0),
        "order": with_ends(jax.random.randint(splits[3], (STEPS,), 0, NBLK), jax.random.fold_in(splits[3], 1), 0, NBLK - 1).astype(jnp.int32),
        "rate": jnp.clip(jnp.exp(jax.random.uniform(splits[4], (NBLK,), jnp.float32, math.log(0.1), math.log(0.4))), 0.1, 0.4),
        "penalty": jnp.clip(jax.random.uniform(splits[5], (NBLK,), jnp.float32, 0.4, 1.2), 0.4, 1.2),
    }


def reference(acts, residual, weights, order, rate, penalty):
    scale = math.sqrt(CH)
    thresh_unit = math.sqrt(D)
    eta_unit = float(CH) / float(TOKENS)
    state = weights.astype(jnp.float32)
    resid = residual
    for step in range(STEPS):
        which = order[step].astype(jnp.int32)
        start = (which * BLOCK).astype(jnp.int32)
        block_acts = lax.dynamic_slice_in_dim(acts, start, BLOCK, 1)
        lowered = resid.astype(jnp.bfloat16)
        grad = lax.dot_general(block_acts, lowered, (((0,), (0,)), ((), ())), preferred_element_type=jnp.float32) / scale
        current = lax.dynamic_index_in_dim(state, which, 0, keepdims=False)
        shifted = current - rate[which] * eta_unit * grad
        sums = lax.optimization_barrier(jnp.sum(shifted * shifted, axis=1))
        factor = jnp.maximum(0.0, 1.0 - penalty[which] * thresh_unit / jnp.sqrt(sums + 1e-06))
        fresh = factor[:, None] * shifted
        change = (fresh - current).astype(jnp.bfloat16)
        state = lax.dynamic_update_index_in_dim(state, fresh, which, 0)
        resid = resid + jnp.dot(block_acts, change, preferred_element_type=jnp.float32) / scale
    return (state, resid)
```

```python
import math

import jax
import jax.numpy as jnp
from jax import lax
from jax.experimental import pallas as pl
from jax.experimental.pallas import tpu as pltpu
from jax.sharding import PartitionSpec as P

D = 8192
CH = 28672
STEPS = 4
NBLK = 32
BLOCK = 896
TOKENS = 8192
NZ = 16
NCOL = 32
ROWS = BLOCK // NZ
COLS = D // NCOL
PIECE = TOKENS // NZ // NCOL
HALF = COLS // 2
CHUNK = (2 * ROWS, HALF)
FAR = (0, 4, -4, 8)
FAR_ORDER = (3, 1, 2)
MESH = pl.DeviceIdType.MESH
F32 = jnp.float32
BF16 = jnp.bfloat16


def fold(rows):
    return jnp.concatenate([rows[:, :HALF], rows[:, HALF:]], axis=0)


def unfold(chunk):
    wide = chunk.astype(F32)
    return jnp.concatenate([wide[:ROWS], wide[ROWS:]], axis=1)


def kernel(
    order_ref, rate_ref, penalty_ref, acts_ref, resid_ref, weights_ref,
    fresh_ref, out_ref,
    pieces, blocks, grad, near_out, near_in, far_out, far_in, sums, gathered, change,
    a2a_s, a2a_r, line_s, line_r, plane_s, plane_r, twin_s, twin_r,
    rn_s, rn_r, rf_s, rf_r, sum_s, sum_r, gf_s, gf_r, gn_s, gn_r,
):
    z = lax.axis_index("tok")
    q = lax.axis_index("col")
    core = lax.rem(q, 2)
    y = lax.rem(q // 2, 4)
    x = q // 8
    near = (0, 1, -1, 2 - 4 * core)
    pending = []

    def at_z(offset):
        return {"tok": lax.rem(z + offset + 2 * NZ, NZ)}

    def at_col(i):
        return {"col": lax.rem(q + i, NCOL)}

    def send(src, dst, ssem, rsem, where):
        copy = pltpu.make_async_remote_copy(
            src_ref=src, dst_ref=dst, send_sem=ssem, recv_sem=rsem, device_id=where, device_id_type=MESH
        )
        copy.start()
        pending.append(copy)
        return copy

    barrier = pltpu.get_barrier_semaphore()

    @pl.loop(1, NCOL)
    def _(i):
        pl.semaphore_signal(barrier, inc=1, device_id=at_col(i), device_id_type=MESH)

    for offset in (1, -1, 2, -2, 4, -4, 8):
        pl.semaphore_signal(barrier, inc=1, device_id=at_z(offset), device_id_type=MESH)
    pl.semaphore_wait(barrier, NCOL - 1 + 7)

    def piece_copy(i):
        peer = lax.rem(q + i, NCOL)
        return pltpu.make_async_remote_copy(
            src_ref=acts_ref.at[pl.ds(pl.multiple_of(peer * PIECE, PIECE), PIECE)],
            dst_ref=pieces.at[q],
            send_sem=a2a_s.at[i],
            recv_sem=a2a_r.at[i],
            device_id=at_col(i),
            device_id_type=MESH,
        )

    @pl.loop(1, NCOL)
    def _(i):
        piece_copy(i).start()

    pieces[q] = acts_ref[pl.ds(pl.multiple_of(q * PIECE, PIECE), PIECE), :]
    out_ref[...] = resid_ref[...]

    @pl.loop(1, NCOL)
    def _(i):
        piece_copy(i).wait()

    def peer_x(i):
        return {"col": (lax.rem(x + i, 4) * 4 + y) * 2 + core}

    def peer_y(i):
        return {"col": (x * 4 + lax.rem(y + i, 4)) * 2 + core}

    for k in range(STEPS):
        blocks[k, x, y, core] = pieces[order_ref[k]]
    line = {}
    for k in range(STEPS):
        mine = blocks.at[k, x, y, core]
        first = peer_x if k % 2 == 0 else peer_y
        line[k] = [send(mine, mine, line_s.at[k, i], line_r.at[k, i], first(i)) for i in (1, 3, 2)]

    plane, twin = {}, {}

    def start_plane(k):
        for copy in line[k]:
            copy.wait_recv()
        mine = blocks.at[k, :, y, core] if k % 2 == 0 else blocks.at[k, x, :, core]
        second = peer_y if k % 2 == 0 else peer_x
        plane[k] = [send(mine, mine, plane_s.at[k, i], plane_r.at[k, i], second(i)) for i in (1, 3, 2)]

    def start_twin(k):
        for copy in plane[k]:
            copy.wait_recv()
        mine = blocks.at[k, :, :, core]
        twin[k] = send(mine, mine, twin_s.at[k], twin_r.at[k], {"col": q + 1 - 2 * core})

    start_plane(0)
    start_plane(1)
    start_twin(0)

    scale = math.sqrt(CH)
    eta_unit = float(CH) / float(TOKENS)
    thresh_unit = math.sqrt(D)
    for k in range(STEPS):
        twin[k].wait_recv()
        block_acts = blocks[k].reshape(TOKENS // NZ, BLOCK)
        lowered = out_ref[...].astype(BF16)
        grad[...] = lax.dot_general(
            block_acts, lowered, (((0,), (0,)), ((), ())), preferred_element_type=F32
        )

        def partial(a, b):
            owner = lax.rem(z + FAR[a] + near[b] + 2 * NZ, NZ)
            return fold(grad[pl.ds(pl.multiple_of(owner * ROWS, 8), ROWS), :])

        near_copies, far_copies = {}, []
        for a in FAR_ORDER + (0,):
            for b in (1, 2, 3):
                near_out[k, a, b] = partial(a, b).astype(BF16)
                near_copies[a, b] = send(
                    near_out.at[k, a, b], near_in.at[k, a, b], rn_s.at[k, a, b], rn_r.at[k, a, b], at_z(near[b])
                )
        if k + 2 < STEPS:
            start_plane(k + 2)
        if k + 1 < STEPS:
            start_twin(k + 1)
        for a in FAR_ORDER + (0,):
            total = partial(a, 0)
            for b in (1, 2, 3):
                near_copies[a, b].wait_recv()
                total = total + near_in[k, a, b].astype(F32)
            if a:
                far_out[k, a] = total.astype(BF16)
                far_copies.append(
                    send(far_out.at[k, a], far_in.at[k, a], rf_s.at[k, a], rf_r.at[k, a], at_z(FAR[a]))
                )
        for a, copy in zip(FAR_ORDER, far_copies):
            copy.wait_recv()
            total = total + far_in[k, a].astype(F32)
        mean_grad = jnp.concatenate([total[:ROWS], total[ROWS:]], axis=1) / scale

        which = order_ref[k]
        current = weights_ref[which].astype(F32)
        for j in range(k):
            current = jnp.where(order_ref[j] == which, fresh_ref[j], current)
        shifted = current - (rate_ref[which] * eta_unit) * mean_grad
        square = shifted * shifted
        square = square[:, :HALF] + square[:, HALF:]
        square = jnp.concatenate([square, jnp.zeros((HALF - ROWS, HALF), F32)], axis=0)
        sums[k, q] = jnp.broadcast_to(jnp.sum(square.T, axis=0, keepdims=True), (8, HALF))

        def sum_copy(i):
            return pltpu.make_async_remote_copy(
                src_ref=sums.at[k, q],
                dst_ref=sums.at[k, q],
                send_sem=sum_s.at[k, i],
                recv_sem=sum_r.at[k, i],
                device_id=at_col(i),
                device_id_type=MESH,
            )

        @pl.loop(1, NCOL)
        def _(i):
            sum_copy(i).start()

        @pl.loop(1, NCOL)
        def _(i):
            sum_copy(i).wait()

        whole = jnp.sum(sums[k], axis=0)
        limit = penalty_ref[which] * thresh_unit
        factor = jnp.maximum(0.0, 1.0 - limit / jnp.sqrt(whole + 1e-06))
        factor = jnp.broadcast_to(factor[:1], (HALF, HALF)).T[:ROWS]
        fresh = jnp.concatenate([factor, factor], axis=1) * shifted
        fresh_ref[k] = fresh

        gathered[k, 0, 0] = fold(fresh - current).astype(BF16)
        mine = gathered.at[k, 0, 0]
        far_moves = {
            a: send(mine, gathered.at[k, a, 0], gf_s.at[k, a], gf_r.at[k, a], at_z(FAR[a])) for a in FAR_ORDER
        }
        near_moves = []
        for a in (0, 1, 2, 3):
            if a:
                far_moves[a].wait_recv()
            for b in (1, 2, 3):
                near_moves.append(
                    send(
                        gathered.at[k, a, 0], gathered.at[k, a, b], gn_s.at[k, a, b], gn_r.at[k, a, b], at_z(near[b])
                    )
                )
        for copy in near_moves:
            copy.wait_recv()
        for a in range(4):
            for b in range(4):
                source = lax.rem(z - FAR[a] - near[b] + 2 * NZ, NZ)
                change[pl.ds(pl.multiple_of(source * ROWS, 8), ROWS), :] = unfold(gathered[k, a, b])
        out_ref[...] = out_ref[...] + (
            jnp.dot(block_acts, change[...].astype(BF16), preferred_element_type=F32) / scale
        )
    for copy in pending:
        copy.wait_send()


def place_kernel(order_ref, weights_ref, fresh_ref, out_ref):
    out_ref[...] = weights_ref[...].astype(F32)
    for k in range(STEPS):
        out_ref[order_ref[k]] = fresh_ref[k]


def body(acts, residual, weights, order, rate, penalty):
    smem = pl.BlockSpec(memory_space=pltpu.SMEM)
    vmem = pl.BlockSpec(memory_space=pltpu.VMEM)
    sems = pltpu.SemaphoreType.DMA
    fresh, resid = pl.pallas_call(
        kernel,
        out_shape=(
            jax.ShapeDtypeStruct((STEPS, ROWS, COLS), F32),
            jax.ShapeDtypeStruct(residual.shape, F32),
        ),
        in_specs=[smem, smem, smem, vmem, vmem, vmem],
        out_specs=(vmem, vmem),
        scratch_shapes=[
            pltpu.VMEM((NCOL, PIECE, BLOCK), BF16),
            pltpu.VMEM((STEPS, 4, 4, 2, PIECE, BLOCK), BF16),
            pltpu.VMEM((BLOCK, COLS), F32),
            pltpu.VMEM((STEPS, 4, 4) + CHUNK, BF16),
            pltpu.VMEM((STEPS, 4, 4) + CHUNK, BF16),
            pltpu.VMEM((STEPS, 4) + CHUNK, BF16),
            pltpu.VMEM((STEPS, 4) + CHUNK, BF16),
            pltpu.VMEM((STEPS, NCOL, 8, HALF), F32),
            pltpu.VMEM((STEPS, 4, 4) + CHUNK, BF16),
            pltpu.VMEM((BLOCK, COLS), F32),
            sems((NCOL,)), sems((NCOL,)),
            sems((STEPS, 4)), sems((STEPS, 4)), sems((STEPS, 4)), sems((STEPS, 4)),
            sems((STEPS,)), sems((STEPS,)),
            sems((STEPS, 4, 4)), sems((STEPS, 4, 4)), sems((STEPS, 4)), sems((STEPS, 4)),
            sems((STEPS, NCOL)), sems((STEPS, NCOL)),
            sems((STEPS, 4)), sems((STEPS, 4)), sems((STEPS, 4, 4)), sems((STEPS, 4, 4)),
        ],
        compiler_params=pltpu.CompilerParams(
            collective_id=0, has_side_effects=True, vmem_limit_bytes=48 * 1024 * 1024
        ),
        name="steps",
    )(order, rate, penalty, acts, residual, weights)
    pruned = pl.pallas_call(
        place_kernel,
        out_shape=jax.ShapeDtypeStruct(weights.shape, F32),
        in_specs=[smem, vmem, vmem],
        out_specs=vmem,
        compiler_params=pltpu.CompilerParams(vmem_limit_bytes=16 * 1024 * 1024),
        name="place",
    )(order, weights, fresh)
    return (pruned, resid)


def solution(mesh):
    in_specs = (P("tok", "col"), P("tok", "col"), P(None, "tok", "col"), P(), P(), P())
    out_specs = (P(None, "tok", "col"), P("tok", "col"))
    return jax.shard_map(body, mesh=mesh, in_specs=in_specs, out_specs=out_specs, check_vma=False)
```

```python
import math

import jax
import jax.numpy as jnp
from jax import lax
from jax.experimental import pallas as pl
from jax.experimental.pallas import tpu as pltpu
from jax.sharding import PartitionSpec as P

D = 8192
CH = 28672
STEPS = 4
NBLK = 32
BLOCK = 896
TOKENS = 8192
NZ = 16
NCOL = 32
ROWS = BLOCK // NZ
COLS = D // NCOL
PIECE = TOKENS // NZ // NCOL
HALF = COLS // 2
CHUNK = (2 * ROWS, HALF)
FAR = (0, 4, -4, 8)
FAR_ORDER = (3, 1, 2)
MESH = pl.DeviceIdType.MESH
F32 = jnp.float32
BF16 = jnp.bfloat16


def fold(rows):
    return jnp.concatenate([rows[:, :HALF], rows[:, HALF:]], axis=0)


def unfold(chunk):
    wide = chunk.astype(F32)
    return jnp.concatenate([wide[:ROWS], wide[ROWS:]], axis=1)


def kernel(
    order_hbm, rate_hbm, penalty_hbm, acts_ref, resid_ref, weights_hbm,
    fresh_ref, out_ref,
    order_ref, rate_ref, penalty_ref, weights_ref,
    pieces, blocks, grad, near_out, near_in, far_out, far_in, sums, gathered, change,
    load_sems, a2a_r, line_r, plane_r, twin_r, near_r, far_r, sum_r, gf_r, gn_r,
    a2a_s, line_s, plane_s, twin_s, near_s, far_s, sum_s, gf_s, gn_s,
):
    z = lax.axis_index("tok")
    q = lax.axis_index("col")
    core = lax.rem(q, 2)
    y = lax.rem(q // 2, 4)
    x = q // 8
    near = (0, 1, -1, 2 - 4 * core)

    def at_z(offset):
        return {"tok": lax.rem(z + offset + 2 * NZ, NZ)}

    def at_col(i):
        return {"col": lax.rem(q + i, NCOL)}

    def send(src, dst, ssem, rsem, where):
        copy = pltpu.make_async_remote_copy(
            src_ref=src, dst_ref=dst, send_sem=ssem, recv_sem=rsem, device_id=where, device_id_type=MESH
        )
        copy.start()
        return copy

    def recv(ref, sem):
        pltpu.make_async_remote_copy(ref, ref, a2a_s, sem, device_id=at_z(1), device_id_type=MESH).wait_recv()

    def sent(ref, sem):
        pltpu.make_async_remote_copy(ref, ref, sem, a2a_r, device_id=at_z(1), device_id_type=MESH).wait_send()

    own_rows = pl.ds(pl.multiple_of(q * PIECE, PIECE), PIECE)
    loads = [
        pltpu.make_async_copy(src, dst, load_sems.at[i])
        for i, (src, dst) in enumerate((
            (acts_ref.at[own_rows], pieces.at[q]),
            (order_hbm, order_ref),
            (rate_hbm, rate_ref),
            (penalty_hbm, penalty_ref),
            (resid_ref, out_ref),
            (weights_hbm, weights_ref),
        ))
    ]
    for copy in loads:
        copy.start()

    barrier = pltpu.get_barrier_semaphore()

    @pl.loop(1, NCOL)
    def _(i):
        pl.semaphore_signal(barrier, inc=1, device_id=at_col(i), device_id_type=MESH)

    for offset in (1, -1, 2, -2, 4, -4, 8):
        pl.semaphore_signal(barrier, inc=1, device_id=at_z(offset), device_id_type=MESH)
    pl.semaphore_wait(barrier, NCOL - 1 + 7)

    def piece_copy(i):
        peer = lax.rem(q + i, NCOL)
        return pltpu.make_async_remote_copy(
            src_ref=acts_ref.at[pl.ds(pl.multiple_of(peer * PIECE, PIECE), PIECE)],
            dst_ref=pieces.at[q],
            send_sem=a2a_s,
            recv_sem=a2a_r,
            device_id=at_col(i),
            device_id_type=MESH,
        )

    @pl.loop(1, NCOL)
    def _(i):
        piece_copy(i).start()

    for copy in loads:
        copy.wait()
    recv(pieces.at[pl.ds(0, NCOL - 1)], a2a_r)

    def peer_x(i):
        return {"col": (lax.rem(x + i, 4) * 4 + y) * 2 + core}

    def peer_y(i):
        return {"col": (x * 4 + lax.rem(y + i, 4)) * 2 + core}

    for k in range(STEPS):
        blocks[k, x, y, core] = pieces[order_ref[k]]
    for k in range(STEPS):
        mine = blocks.at[k, x, y, core]
        first = peer_x if k % 2 == 0 else peer_y
        for i in (1, 3, 2):
            send(mine, mine, line_s, line_r.at[k], first(i))

    def start_plane(k):
        recv(blocks.at[k, 0:3, 0, 0], line_r.at[k])
        mine = blocks.at[k, :, y, core] if k % 2 == 0 else blocks.at[k, x, :, core]
        second = peer_y if k % 2 == 0 else peer_x
        for i in (1, 3, 2):
            send(mine, mine, plane_s, plane_r.at[k], second(i))

    def start_twin(k):
        recv(blocks.at[k, 0:3, :, 0], plane_r.at[k])
        mine = blocks.at[k, :, :, core]
        send(mine, mine, twin_s, twin_r.at[k], {"col": q + 1 - 2 * core})

    start_plane(0)
    start_plane(1)
    start_twin(0)

    scale = math.sqrt(CH)
    eta_unit = float(CH) / float(TOKENS)
    thresh_unit = math.sqrt(D)
    for k in range(STEPS):
        recv(blocks.at[k, :, :, 0], twin_r.at[k])
        block_acts = blocks[k].reshape(TOKENS // NZ, BLOCK)
        lowered = out_ref[...].astype(BF16)
        grad[...] = lax.dot_general(
            block_acts, lowered, (((0,), (0,)), ((), ())), preferred_element_type=F32
        )

        def partial(a, b):
            owner = lax.rem(z + FAR[a] + near[b] + 2 * NZ, NZ)
            return fold(grad[pl.ds(pl.multiple_of(owner * ROWS, 8), ROWS), :])

        for a in FAR_ORDER + (0,):
            for b in (1, 2, 3):
                near_out[k, a, b - 1] = partial(a, b).astype(BF16)
                send(near_out.at[k, a, b - 1], near_in.at[k, a, b - 1], near_s, near_r.at[k, a], at_z(near[b]))
        if k + 2 < STEPS:
            start_plane(k + 2)
        if k + 1 < STEPS:
            start_twin(k + 1)
        for a in FAR_ORDER + (0,):
            total = partial(a, 0)
            recv(near_in.at[k, a], near_r.at[k, a])
            for b in range(3):
                total = total + near_in[k, a, b].astype(F32)
            if a:
                far_out[k, a - 1] = total.astype(BF16)
                send(far_out.at[k, a - 1], far_in.at[k, a - 1], far_s, far_r.at[k], at_z(FAR[a]))
        recv(far_in.at[k], far_r.at[k])
        for a in range(3):
            total = total + far_in[k, a].astype(F32)
        mean_grad = jnp.concatenate([total[:ROWS], total[ROWS:]], axis=1) / scale

        which = order_ref[k]
        current = weights_ref[which].astype(F32)
        for j in range(k):
            current = jnp.where(order_ref[j] == which, fresh_ref[j], current)
        shifted = current - (rate_ref[which] * eta_unit) * mean_grad
        square = shifted * shifted
        square = square[:, :HALF] + square[:, HALF:]
        square = jnp.concatenate([square, jnp.zeros((HALF - ROWS, HALF), F32)], axis=0)
        sums[k, q] = jnp.sum(square.T, axis=0, keepdims=True)

        def sum_copy(i):
            return pltpu.make_async_remote_copy(
                src_ref=sums.at[k, q],
                dst_ref=sums.at[k, q],
                send_sem=sum_s,
                recv_sem=sum_r.at[k],
                device_id=at_col(i),
                device_id_type=MESH,
            )

        @pl.loop(1, NCOL)
        def _(i):
            sum_copy(i).start()

        recv(sums.at[k, pl.ds(0, NCOL - 1)], sum_r.at[k])
        whole = jnp.sum(sums[k], axis=0)
        limit = penalty_ref[which] * thresh_unit
        factor = jnp.maximum(0.0, 1.0 - limit / jnp.sqrt(whole + 1e-06))
        factor = jnp.broadcast_to(factor, (HALF, HALF)).T[:ROWS]
        fresh = jnp.concatenate([factor, factor], axis=1) * shifted
        fresh_ref[k] = fresh

        gathered[k, 0, 0] = fold(fresh - current).astype(BF16)
        mine = gathered.at[k, 0, 0]
        for a in FAR_ORDER:
            send(mine, gathered.at[k, a, 0], gf_s, gf_r.at[k, a - 1], at_z(FAR[a]))
        for a in (0, 1, 2, 3):
            if a:
                recv(gathered.at[k, a, 0], gf_r.at[k, a - 1])
            for b in (1, 2, 3):
                send(gathered.at[k, a, 0], gathered.at[k, a, b], gn_s, gn_r.at[k], at_z(near[b]))
        recv(gathered.at[k, :, 1:4], gn_r.at[k])
        for a in range(4):
            for b in range(4):
                source = lax.rem(z - FAR[a] - near[b] + 2 * NZ, NZ)
                change[pl.ds(pl.multiple_of(source * ROWS, 8), ROWS), :] = unfold(gathered[k, a, b])
        out_ref[...] = out_ref[...] + (
            jnp.dot(block_acts, change[...].astype(BF16), preferred_element_type=F32) / scale
        )
    sent(pieces.at[pl.ds(0, NCOL - 1)], a2a_s)
    sent(blocks.at[:, 0:3, 0, 0], line_s)
    sent(blocks.at[:, 0:3, :, 0], plane_s)
    sent(blocks.at[:, :, :, 0], twin_s)
    sent(near_out, near_s)
    sent(far_out, far_s)
    sent(sums.at[:, pl.ds(0, NCOL - 1)], sum_s)
    sent(gathered.at[:, 1:4, 0], gf_s)
    sent(gathered.at[:, :, 1:4], gn_s)


def place_kernel(order_ref, weights_ref, fresh_ref, out_ref):
    out_ref[...] = weights_ref[...].astype(F32)
    for k in range(STEPS):
        out_ref[order_ref[k]] = fresh_ref[k]


def body(acts, residual, weights, order, rate, penalty):
    smem = pl.BlockSpec(memory_space=pltpu.SMEM)
    vmem = pl.BlockSpec(memory_space=pltpu.VMEM)
    hbm = pl.BlockSpec(memory_space=pl.ANY)
    one = pltpu.SemaphoreType.DMA(())
    sems = pltpu.SemaphoreType.DMA
    fresh, resid = pl.pallas_call(
        kernel,
        out_shape=(
            jax.ShapeDtypeStruct((STEPS, ROWS, COLS), F32),
            jax.ShapeDtypeStruct(residual.shape, F32),
        ),
        in_specs=[hbm] * 6,
        out_specs=(vmem, vmem),
        scratch_shapes=[
            pltpu.SMEM((STEPS,), jnp.int32),
            pltpu.SMEM((NBLK,), F32),
            pltpu.SMEM((NBLK,), F32),
            pltpu.VMEM(weights.shape, BF16),
            pltpu.VMEM((NCOL, PIECE, BLOCK), BF16),
            pltpu.VMEM((STEPS, 4, 4, 2, PIECE, BLOCK), BF16),
            pltpu.VMEM((BLOCK, COLS), F32),
            pltpu.VMEM((STEPS, 4, 3) + CHUNK, BF16),
            pltpu.VMEM((STEPS, 4, 3) + CHUNK, BF16),
            pltpu.VMEM((STEPS, 3) + CHUNK, BF16),
            pltpu.VMEM((STEPS, 3) + CHUNK, BF16),
            pltpu.VMEM((STEPS, NCOL, 1, HALF), F32),
            pltpu.VMEM((STEPS, 4, 4) + CHUNK, BF16),
            pltpu.VMEM((BLOCK, COLS), F32),
            sems((6,)),
            one, sems((STEPS,)), sems((STEPS,)), sems((STEPS,)), sems((STEPS, 4)),
            sems((STEPS,)), sems((STEPS,)), sems((STEPS, 3)), sems((STEPS,)),
            one, one, one, one, one, one, one, one, one,
        ],
        compiler_params=pltpu.CompilerParams(
            collective_id=0, has_side_effects=True, vmem_limit_bytes=62 * 1024 * 1024
        ),
        name="steps",
    )(order, rate, penalty, acts, residual, weights)
    pruned = pl.pallas_call(
        place_kernel,
        out_shape=jax.ShapeDtypeStruct(weights.shape, F32),
        in_specs=[smem, vmem, vmem],
        out_specs=vmem,
        compiler_params=pltpu.CompilerParams(vmem_limit_bytes=16 * 1024 * 1024),
        name="place",
    )(order, weights, fresh)
    return (pruned, resid)


def solution(mesh):
    in_specs = (P("tok", "col"), P("tok", "col"), P(None, "tok", "col"), P(), P(), P())
    out_specs = (P(None, "tok", "col"), P("tok", "col"))
    return jax.shard_map(body, mesh=mesh, in_specs=in_specs, out_specs=out_specs, check_vma=False)
```

```python
import math

import jax
import jax.numpy as jnp
from jax import lax
from jax.experimental import pallas as pl
from jax.experimental.pallas import tpu as pltpu
from jax.sharding import PartitionSpec as P

D = 8192
CH = 28672
STEPS = 4
NBLK = 32
BLOCK = 896
TOKENS = 8192
NZ = 16
NCOL = 32
ROWS = BLOCK // NZ
COLS = D // NCOL
PIECE = TOKENS // NZ // NCOL
HALF = COLS // 2
CHUNK = (2 * ROWS, HALF)
FAR = (0, 3, -3, 6, -6)
FAR_ORDER = (3, 4, 1, 2)
NEAR = (0, 1, -1)
CUT = 48
SETS = STEPS + 2
TILES = BLOCK // HALF
PAIR = {(1, 0): 0, (2, 0): 1, (2, 1): 2, (3, 0): 3, (3, 1): 4, (3, 2): 5}
GRAM_COUNT = ((TILES + 1) // 2, (5 * TILES + 1) // 2)
GRAM_AT = (0, GRAM_COUNT[0])
GRAM_SPOT = (GRAM_COUNT[1], 0)
MESH = pl.DeviceIdType.MESH
F32 = jnp.float32
BF16 = jnp.bfloat16


def fold(rows):
    return jnp.concatenate([rows[:, :HALF], rows[:, HALF:]], axis=0)


def unfold(chunk):
    wide = chunk.astype(F32)
    return jnp.concatenate([wide[:ROWS], wide[ROWS:]], axis=1)


def kernel(
    order_hbm, rate_hbm, penalty_hbm, acts_ref, resid_ref, weights_hbm,
    fresh_ref, out_ref,
    order_ref, rate_ref, penalty_ref, weights_ref, lowered,
    pieces, blocks, source, near_out, near_in, across_out, across_in, near_sum, far_out, far_in, sums, gathered, opposite, change, delta,
    gram_in, gram,
    load_sems, a2a_r, line_r, plane_r, twin_r, near_r, across_r, far_r, sum_r, gf_r, gn_r, go_r, gram_r,
    a2a_s, line_s, plane_s, twin_s, near_s, across_s, far_s, sum_s, gf_s, gn_s, go_s, gram_s,
):
    z = lax.axis_index("tok")
    q = lax.axis_index("col")
    core = lax.rem(q, 2)
    y = lax.rem(q // 2, 4)
    x = q // 8
    spot = q // 2 + NCOL // 2 * core

    def at_z(offset):
        return {"tok": lax.rem(z + offset + 2 * NZ, NZ)}

    def at_col(i):
        return {"col": lax.rem(q + i, NCOL)}

    def remote(src, dst, ssem, rsem, where):
        return pltpu.make_async_remote_copy(
            src_ref=src, dst_ref=dst, send_sem=ssem, recv_sem=rsem, device_id=where, device_id_type=MESH
        )

    def send(src, dst, ssem, rsem, where):
        remote(src, dst, ssem, rsem, where).start()

    def recv(ref, sem):
        remote(ref, ref, a2a_s, sem, at_z(1)).wait_recv()

    def sent(ref, sem):
        remote(ref, ref, sem, a2a_r, at_z(1)).wait_send()

    own_rows = pl.ds(pl.multiple_of(q * PIECE, PIECE), PIECE)
    loads = [
        pltpu.make_async_copy(src, dst, load_sems.at[i])
        for i, (src, dst) in enumerate((
            (acts_ref.at[own_rows], pieces.at[q]),
            (order_hbm, order_ref),
            (rate_hbm, rate_ref),
            (penalty_hbm, penalty_ref),
            (resid_ref, out_ref),
            (weights_hbm, weights_ref),
        ))
    ]
    for copy in loads:
        copy.start()

    barrier = pltpu.get_barrier_semaphore()

    @pl.loop(1, NCOL)
    def _(i):
        pl.semaphore_signal(barrier, inc=1, device_id=at_col(i), device_id_type=MESH)

    for offset in (1, -1, 2, -2, 3, -3, 6, -6):
        pl.semaphore_signal(barrier, inc=1, device_id=at_z(offset), device_id_type=MESH)
    pl.semaphore_wait(barrier, NCOL - 1 + 8)

    @pl.loop(1, NCOL)
    def _(i):
        peer = lax.rem(q + i, NCOL)
        rows = pl.ds(pl.multiple_of(peer * PIECE, PIECE), PIECE)
        send(acts_ref.at[rows], pieces.at[q], a2a_s, a2a_r, at_col(i))

    for copy in loads:
        copy.wait()
    lowered[...] = out_ref[...].astype(BF16)
    recv(pieces.at[pl.ds(0, NCOL - 1)], a2a_r)

    def peer_x(i):
        return {"col": (lax.rem(x + i, 4) * 4 + y) * 2 + core}

    def peer_y(i):
        return {"col": (x * 4 + lax.rem(y + i, 4)) * 2 + core}

    for k in range(STEPS):
        blocks[k, x, y, core] = pieces[order_ref[k]]
    first_piece = blocks.at[0, x, y, core]

    @pl.loop(1, NCOL // 2)
    def _(i):
        send(first_piece, first_piece, line_s.at[0], line_r.at[0], {"col": lax.rem(q + 2 * i, NCOL)})

    for k in range(1, STEPS):
        mine = blocks.at[k, x, y, core]
        first = peer_x if k % 2 == 0 else peer_y
        for i in (1, 3, 2):
            send(mine, mine, line_s.at[1], line_r.at[k], first(i))

    def start_plane(k):
        recv(blocks.at[k, 0:3, 0, 0], line_r.at[k])
        mine = blocks.at[k, :, y, core] if k % 2 == 0 else blocks.at[k, x, :, core]
        second = peer_y if k % 2 == 0 else peer_x
        for i in (1, 3, 2):
            send(mine, mine, plane_s, plane_r.at[k], second(i))

    def start_twin(k):
        if k == 0:
            recv(pieces.at[pl.ds(0, NCOL // 2 - 1)], line_r.at[0])
        else:
            recv(blocks.at[k, 0:3, :, 0], plane_r.at[k])
        mine = blocks.at[k, :, :, core]
        send(mine, mine, twin_s, twin_r.at[k], {"col": q + 1 - 2 * core})

    def ready(k):
        recv(blocks.at[k, :, :, 0], twin_r.at[k])

    def block_acts(k):
        return blocks[k].reshape(TOKENS // NZ, BLOCK)

    def over_tokens(a, b):
        return lax.dot_general(a, b, (((0,), (0,)), ((), ())), preferred_element_type=F32)

    def partial(s, offset):
        owner = lax.rem(z + offset + 2 * NZ, NZ)
        return fold(source[s, pl.ds(pl.multiple_of(owner * ROWS, 8), ROWS), :])

    def sum_kind(s):
        return max(0, s - 3)

    halves = ((pl.ds(0, CUT), 2), (pl.ds(CUT, CHUNK[0] - CUT), -2))

    def sum_start(s):
        kind = sum_kind(s)
        across_out[s] = partial(s, NZ // 2).astype(BF16)
        for i, (rows, offset) in enumerate(halves):
            send(
                across_out.at[s, rows], across_in.at[s, rows], across_s.at[kind], across_r.at[s, i], at_z(offset)
            )
        for a in FAR_ORDER + (0,):
            for b in (1, 2):
                near_out[s, a, b - 1] = partial(s, FAR[a] + NEAR[b]).astype(BF16)
                send(
                    near_out.at[s, a, b - 1], near_in.at[s, a, b - 1],
                    near_s.at[kind], near_r.at[s, a], at_z(NEAR[b]),
                )

    def sum_middle(s):
        kind = sum_kind(s)
        for a in FAR_ORDER + (0,):
            total = partial(s, FAR[a])
            recv(near_in.at[s, a], near_r.at[s, a])
            for b in range(2):
                total = total + near_in[s, a, b].astype(F32)
            if a == 3:
                recv(across_in.at[s, 0:CUT], across_r.at[s, 0])
                top = total[:CUT] + across_in[s, 0:CUT].astype(F32)
                total = jnp.concatenate([top, total[CUT:]], axis=0)
            if a == 4:
                recv(across_in.at[s, CUT : CHUNK[0]], across_r.at[s, 1])
                low = total[CUT:] + across_in[s, CUT : CHUNK[0]].astype(F32)
                total = jnp.concatenate([total[:CUT], low], axis=0)
            if a:
                far_out[s, a - 1] = total.astype(BF16)
                send(far_out.at[s, a - 1], far_in.at[s, a - 1], far_s.at[kind], far_r.at[s], at_z(FAR[a]))
            else:
                near_sum[s] = total

    def sum_end(s):
        recv(far_in.at[s], far_r.at[s])
        total = near_sum[s]
        for a in range(4):
            total = total + far_in[s, a].astype(F32)
        return total

    def gradient(k):
        source[k] = over_tokens(block_acts(k), lowered[...])
        sum_start(k)

    def tile(k, t):
        lanes = pl.ds(pl.multiple_of(t * HALF, HALF), HALF)
        return blocks[k, :, :, :, :, lanes].reshape(TOKENS // NZ, HALF)

    def gram_first():
        for h in range(2):
            source[4, :, h * HALF : (h + 1) * HALF] = over_tokens(block_acts(1), tile(0, lax.rem(2 * (spot - GRAM_SPOT[0]) + h, TILES)))
        sum_start(4)

    def gram_rest():
        for h in range(2):
            item = lax.rem(2 * spot + h, 5 * TILES)
            pair = item // TILES
            later = (pair + 1) // 3
            source[5, :, h * HALF : (h + 1) * HALF] = over_tokens(
                block_acts(2 + later), tile(pair - 2 * later, lax.rem(item, TILES))
            )
        sum_start(5)

    def gram_send(kind):
        at = GRAM_AT[kind] + spot - GRAM_SPOT[kind]
        gram_in[at] = sum_end(4 + kind).astype(BF16)

        @pl.loop(1, NCOL)
        def _(i):
            send(gram_in.at[at], gram_in.at[at], gram_s.at[kind], gram_r.at[kind], at_col(i))

    def gram_recv(kind):
        count = GRAM_COUNT[kind]

        @pl.when(has_gram[kind])
        def _():
            recv(gram_in.at[pl.ds(0, count - 1)], gram_r.at[kind])

        @pl.when(jnp.logical_not(has_gram[kind]))
        def _():
            recv(gram_in.at[pl.ds(0, count)], gram_r.at[kind])

        for item in range((1, 5)[kind] * TILES):
            chunk = gram_in[GRAM_AT[kind] + item // 2].astype(F32)
            at = ROWS * (item % 2)
            lane = HALF * (item % TILES)
            gram[kind + item // TILES, :, lane : lane + HALF] = chunk[at : at + ROWS]

    def correction(k, j):
        return jnp.dot(gram[PAIR[k, j]].astype(BF16), delta[j], preferred_element_type=F32)

    scale = math.sqrt(CH)
    eta_unit = float(CH) / float(TOKENS)
    thresh_unit = math.sqrt(D)

    def shift(k, corrections):
        total = sum_end(k)
        whole = jnp.concatenate([total[:ROWS], total[ROWS:]], axis=1)
        for value in corrections:
            whole = whole + value / scale
        which = order_ref[k]
        current = weights_ref[which].astype(F32)
        for j in range(k):
            current = jnp.where(order_ref[j] == which, fresh_ref[j], current)
        shifted = current - (rate_ref[which] * eta_unit) * (whole / scale)
        square = shifted * shifted
        square = square[:, :HALF] + square[:, HALF:]
        square = jnp.concatenate([square, jnp.zeros((HALF - ROWS, HALF), F32)], axis=0)
        sums[k, q] = jnp.sum(square.T, axis=0, keepdims=True)

        @pl.loop(1, NCOL)
        def _(i):
            send(sums.at[k, q], sums.at[k, q], sum_s, sum_r.at[k], at_col(i))

        return current, shifted

    def shrink(k, current, shifted, meanwhile=None):
        recv(sums.at[k, pl.ds(0, NCOL - 1)], sum_r.at[k])
        whole = jnp.sum(sums[k], axis=0)
        limit = penalty_ref[order_ref[k]] * thresh_unit
        factor = jnp.maximum(0.0, 1.0 - limit / jnp.sqrt(whole + 1e-06))
        factor = jnp.broadcast_to(factor, (HALF, HALF)).T[:ROWS]
        fresh = jnp.concatenate([factor, factor], axis=1) * shifted
        fresh_ref[k] = fresh
        gathered[k, 0, 0] = fold(fresh - current).astype(BF16)
        for a in FAR_ORDER:
            send(gathered.at[k, 0, 0], gathered.at[k, a, 0], gf_s, gf_r.at[k, a - 1], at_z(FAR[a]))
        for b in (1, 2):
            send(gathered.at[k, 0, 0], gathered.at[k, 0, b], gn_s, gn_r.at[k], at_z(NEAR[b]))
        if meanwhile is not None:
            meanwhile()
        for a in range(1, 5):
            recv(gathered.at[k, a, 0], gf_r.at[k, a - 1])
            if a >= 3:
                rows, offset = halves[a - 3]
                send(gathered.at[k, a, 0, rows], opposite.at[k, rows], go_s, go_r.at[k], at_z(offset))
            for b in (1, 2):
                send(gathered.at[k, a, 0], gathered.at[k, a, b], gn_s, gn_r.at[k], at_z(NEAR[b]))

    def collect(k):
        def put(offset, chunk):
            owner = lax.rem(z - offset + 2 * NZ, NZ)
            change[pl.ds(pl.multiple_of(owner * ROWS, 8), ROWS), :] = unfold(chunk)

        for a in range(5):
            put(FAR[a], gathered[k, a, 0])
        recv(gathered.at[k, :, 1:3], gn_r.at[k])
        recv(opposite.at[k], go_r.at[k])
        for a in range(5):
            for b in (1, 2):
                put(FAR[a] + NEAR[b], gathered[k, a, b])
        put(NZ // 2, opposite[k])
        delta[k] = change[...].astype(BF16)

    def update(k):
        out_ref[...] = out_ref[...] + (
            jnp.dot(block_acts(k), delta[k], preferred_element_type=F32) / scale
        )

    has_gram = [
        (spot >= GRAM_SPOT[kind]) & (spot < GRAM_SPOT[kind] + GRAM_COUNT[kind]) for kind in range(2)
    ]

    start_plane(1)
    start_twin(0)
    ready(0)
    gradient(0)
    start_plane(2)
    start_plane(3)
    start_twin(1)
    sum_middle(0)
    ready(1)
    gradient(1)
    pl.when(has_gram[0])(gram_first)
    start_twin(2)
    start_twin(3)

    current, shifted = shift(0, [])
    sum_middle(1)
    pl.when(has_gram[0])(lambda: sum_middle(4))
    shrink(0, current, shifted, lambda: pl.when(has_gram[0])(lambda: gram_send(0)))
    ready(2)
    gradient(2)
    ready(3)
    pl.when(has_gram[1])(gram_rest)
    collect(0)
    gram_recv(0)

    current, shifted = shift(1, [correction(1, 0)])
    update(0)
    sum_middle(2)
    pl.when(has_gram[1])(lambda: sum_middle(5))
    shrink(1, current, shifted, lambda: pl.when(has_gram[1])(lambda: gram_send(1)))
    gradient(3)
    collect(1)
    gram_recv(1)

    current, shifted = shift(2, [correction(2, 0), correction(2, 1)])
    update(1)
    early = [correction(3, 0), correction(3, 1)]
    sum_middle(3)
    shrink(2, current, shifted)
    collect(2)

    current, shifted = shift(3, early + [correction(3, 2)])
    update(2)
    shrink(3, current, shifted)
    collect(3)
    update(3)

    sent(pieces.at[pl.ds(0, NCOL - 1)], a2a_s)
    sent(pieces.at[pl.ds(0, NCOL // 2 - 1)], line_s.at[0])
    sent(blocks.at[1:STEPS, 0:3, 0, 0], line_s.at[1])
    sent(blocks.at[1:STEPS, 0:3, :, 0], plane_s)
    sent(blocks.at[:, :, :, 0], twin_s)
    sent(near_out.at[0:STEPS], near_s.at[0])
    sent(across_out.at[0:STEPS], across_s.at[0])
    sent(far_out.at[0:STEPS], far_s.at[0])
    sent(sums.at[:, pl.ds(0, NCOL - 1)], sum_s)
    sent(gathered.at[:, 1:5, 0], gf_s)
    sent(gathered.at[:, :, 1:3], gn_s)
    sent(opposite, go_s)
    for kind in range(2):

        @pl.when(has_gram[kind])
        def _():
            sent(near_out.at[0], near_s.at[1 + kind])
            sent(across_out.at[0], across_s.at[1 + kind])
            sent(far_out.at[0], far_s.at[1 + kind])
            sent(gram_in.at[pl.ds(0, NCOL - 1)], gram_s.at[kind])


def place_kernel(order_ref, weights_ref, fresh_ref, out_ref):
    out_ref[...] = weights_ref[...].astype(F32)
    for k in range(STEPS):
        out_ref[order_ref[k]] = fresh_ref[k]


def body(acts, residual, weights, order, rate, penalty):
    smem = pl.BlockSpec(memory_space=pltpu.SMEM)
    vmem = pl.BlockSpec(memory_space=pltpu.VMEM)
    hbm = pl.BlockSpec(memory_space=pl.ANY)
    one = pltpu.SemaphoreType.DMA(())
    sems = pltpu.SemaphoreType.DMA
    fresh, resid = pl.pallas_call(
        kernel,
        out_shape=(
            jax.ShapeDtypeStruct((STEPS, ROWS, COLS), F32),
            jax.ShapeDtypeStruct(residual.shape, F32),
        ),
        in_specs=[hbm] * 6,
        out_specs=(vmem, vmem),
        scratch_shapes=[
            pltpu.SMEM((STEPS,), jnp.int32),
            pltpu.SMEM((NBLK,), F32),
            pltpu.SMEM((NBLK,), F32),
            pltpu.VMEM(weights.shape, BF16),
            pltpu.VMEM(residual.shape, BF16),
            pltpu.VMEM((NCOL, PIECE, BLOCK), BF16),
            pltpu.VMEM((STEPS, 4, 4, 2, PIECE, BLOCK), BF16),
            pltpu.VMEM((SETS, BLOCK, COLS), F32),
            pltpu.VMEM((SETS, 5, 2) + CHUNK, BF16),
            pltpu.VMEM((SETS, 5, 2) + CHUNK, BF16),
            pltpu.VMEM((SETS,) + CHUNK, BF16),
            pltpu.VMEM((SETS,) + CHUNK, BF16),
            pltpu.VMEM((SETS,) + CHUNK, F32),
            pltpu.VMEM((SETS, 4) + CHUNK, BF16),
            pltpu.VMEM((SETS, 4) + CHUNK, BF16),
            pltpu.VMEM((STEPS, NCOL, 1, HALF), F32),
            pltpu.VMEM((STEPS, 5, 3) + CHUNK, BF16),
            pltpu.VMEM((STEPS,) + CHUNK, BF16),
            pltpu.VMEM((BLOCK, COLS), F32),
            pltpu.VMEM((STEPS, BLOCK, COLS), BF16),
            pltpu.VMEM((NCOL,) + CHUNK, BF16),
            pltpu.VMEM((len(PAIR), ROWS, BLOCK), F32),
            sems((6,)),
            one, sems((STEPS,)), sems((STEPS,)), sems((STEPS,)), sems((SETS, 5)), sems((SETS, 2)),
            sems((SETS,)), sems((STEPS,)), sems((STEPS, 4)), sems((STEPS,)), sems((STEPS,)), sems((2,)),
            one, sems((2,)), one, one, sems((3,)), sems((3,)), sems((3,)), one, one, one, one, sems((2,)),
        ],
        compiler_params=pltpu.CompilerParams(
            collective_id=0, has_side_effects=True, vmem_limit_bytes=62 * 1024 * 1024
        ),
        name="steps",
    )(order, rate, penalty, acts, residual, weights)
    pruned = pl.pallas_call(
        place_kernel,
        out_shape=jax.ShapeDtypeStruct(weights.shape, F32),
        in_specs=[smem, vmem, vmem],
        out_specs=vmem,
        compiler_params=pltpu.CompilerParams(vmem_limit_bytes=16 * 1024 * 1024),
        name="place",
    )(order, weights, fresh)
    return (pruned, resid)


def solution(mesh):
    in_specs = (P("tok", "col"), P("tok", "col"), P(None, "tok", "col"), P(), P(), P())
    out_specs = (P(None, "tok", "col"), P("tok", "col"))
    return jax.shard_map(body, mesh=mesh, in_specs=in_specs, out_specs=out_specs, check_vma=False)
```

```python
import math

import jax
import jax.numpy as jnp
from jax import lax
from jax.experimental import pallas as pl
from jax.experimental.pallas import tpu as pltpu
from jax.sharding import PartitionSpec as P

D = 8192
CH = 28672
STEPS = 4
NBLK = 32
BLOCK = 896
TOKENS = 8192
NZ = 16
NCOL = 32
ROWS = BLOCK // NZ
COLS = D // NCOL
PIECE = TOKENS // NZ // NCOL
HALF = COLS // 2
EARLY = (3,)
CHUNK = (2 * ROWS, HALF)
FAR = (0, 3, -3, 6, -6)
FAR_ORDER = (3, 4, 1, 2)
NEAR = (0, 1, -1)
CUT = 48
SETS = STEPS + 2
TILES = BLOCK // HALF
PAIR = {(1, 0): 0, (2, 0): 1, (2, 1): 2, (3, 0): 3, (3, 1): 4, (3, 2): 5}
GRAM_COUNT = ((TILES + 1) // 2, (5 * TILES + 1) // 2)
GRAM_AT = (0, GRAM_COUNT[0])
GRAM_SPOT = (GRAM_COUNT[1], 0)
MESH = pl.DeviceIdType.MESH
F32 = jnp.float32
BF16 = jnp.bfloat16


def fold(rows):
    return jnp.concatenate([rows[:, :HALF], rows[:, HALF:]], axis=0)


def unfold(chunk):
    wide = chunk.astype(F32)
    return jnp.concatenate([wide[:ROWS], wide[ROWS:]], axis=1)


def kernel(
    order_hbm, rate_hbm, penalty_hbm, acts_ref, resid_ref, weights_hbm,
    fresh_ref, out_ref,
    order_ref, rate_ref, penalty_ref, weights_ref, lowered,
    pieces, blocks, source, near_out, near_in, across_out, across_in, near_sum, far_out, far_in, sums, gathered, opposite, change, delta, held, factors,
    gram_in, gram,
    load_sems, a2a_r, line_r, plane_r, twin_r, near_r, across_r, far_r, sum_r, gf_r, gn_r, go_r, gram_r, factor_r,
    a2a_s, line_s, plane_s, twin_s, near_s, across_s, far_s, sum_s, gf_s, gn_s, go_s, gram_s, factor_s,
):
    z = lax.axis_index("tok")
    q = lax.axis_index("col")
    core = lax.rem(q, 2)
    y = lax.rem(q // 2, 4)
    x = q // 8
    spot = q // 2 + NCOL // 2 * core

    def at_z(offset):
        return {"tok": lax.rem(z + offset + 2 * NZ, NZ)}

    def at_col(i):
        return {"col": lax.rem(q + i, NCOL)}

    def remote(src, dst, ssem, rsem, where):
        return pltpu.make_async_remote_copy(
            src_ref=src, dst_ref=dst, send_sem=ssem, recv_sem=rsem, device_id=where, device_id_type=MESH
        )

    def send(src, dst, ssem, rsem, where):
        remote(src, dst, ssem, rsem, where).start()

    def recv(ref, sem):
        remote(ref, ref, a2a_s, sem, at_z(1)).wait_recv()

    def sent(ref, sem):
        remote(ref, ref, sem, a2a_r, at_z(1)).wait_send()

    own_rows = pl.ds(pl.multiple_of(q * PIECE, PIECE), PIECE)
    loads = [
        pltpu.make_async_copy(src, dst, load_sems.at[i])
        for i, (src, dst) in enumerate((
            (acts_ref.at[own_rows], pieces.at[q]),
            (order_hbm, order_ref),
            (rate_hbm, rate_ref),
            (penalty_hbm, penalty_ref),
            (resid_ref, out_ref),
            (weights_hbm, weights_ref),
        ))
    ]
    for copy in loads:
        copy.start()

    barrier = pltpu.get_barrier_semaphore()

    @pl.loop(1, NCOL)
    def _(i):
        pl.semaphore_signal(barrier, inc=1, device_id=at_col(i), device_id_type=MESH)

    @pl.loop(1, NZ)
    def _(i):
        pl.semaphore_signal(barrier, inc=1, device_id=at_z(i), device_id_type=MESH)

    pl.semaphore_wait(barrier, NCOL - 1 + NZ - 1)

    halves = ((pl.ds(0, CUT), 2), (pl.ds(CUT, CHUNK[0] - CUT), -2))

    def gather_start(g, rows):
        gathered[g, 0, 0] = fold(rows).astype(BF16)
        for a in FAR_ORDER:
            send(gathered.at[g, 0, 0], gathered.at[g, a, 0], gf_s, gf_r.at[g, a - 1], at_z(FAR[a]))
        for b in (1, 2):
            send(gathered.at[g, 0, 0], gathered.at[g, 0, b], gn_s, gn_r.at[g], at_z(NEAR[b]))

    def gather_forward(g):
        for a in range(1, 5):
            recv(gathered.at[g, a, 0], gf_r.at[g, a - 1])
            if a >= 3:
                rows, offset = halves[a - 3]
                send(gathered.at[g, a, 0, rows], opposite.at[g, rows], go_s, go_r.at[g], at_z(offset))
            for b in (1, 2):
                send(gathered.at[g, a, 0], gathered.at[g, a, b], gn_s, gn_r.at[g], at_z(NEAR[b]))

    def gather_collect(g):
        def put(offset, chunk):
            owner = lax.rem(z - offset + 2 * NZ, NZ)
            change[pl.ds(pl.multiple_of(owner * ROWS, 8), ROWS), :] = unfold(chunk)

        for a in range(5):
            put(FAR[a], gathered[g, a, 0])
        recv(gathered.at[g, :, 1:3], gn_r.at[g])
        recv(opposite.at[g], go_r.at[g])
        for a in range(5):
            for b in (1, 2):
                put(FAR[a] + NEAR[b], gathered[g, a, b])
        put(NZ // 2, opposite[g])

    @pl.loop(1, NCOL)
    def _(i):
        peer = lax.rem(q + i, NCOL)
        rows = pl.ds(pl.multiple_of(peer * PIECE, PIECE), PIECE)
        send(acts_ref.at[rows], pieces.at[q], a2a_s, a2a_r, at_col(i))

    for copy in loads:
        copy.wait()
    lowered[...] = out_ref[...].astype(BF16)
    for k in EARLY:
        gather_start(STEPS + EARLY.index(k), weights_ref[order_ref[k]].astype(F32))
    recv(pieces.at[pl.ds(0, NCOL - 1)], a2a_r)

    def peer_x(i):
        return {"col": (lax.rem(x + i, 4) * 4 + y) * 2 + core}

    def peer_y(i):
        return {"col": (x * 4 + lax.rem(y + i, 4)) * 2 + core}

    for k in range(STEPS):
        blocks[k, x, y, core] = pieces[order_ref[k]]
    first_piece = blocks.at[0, x, y, core]

    @pl.loop(1, NCOL // 2)
    def _(i):
        send(first_piece, first_piece, line_s.at[0], line_r.at[0], {"col": lax.rem(q + 2 * i, NCOL)})

    for k in range(1, STEPS):
        mine = blocks.at[k, x, y, core]
        first = peer_x if k % 2 == 0 else peer_y
        for i in (1, 3, 2):
            send(mine, mine, line_s.at[1], line_r.at[k], first(i))

    def start_plane(k):
        recv(blocks.at[k, 0:3, 0, 0], line_r.at[k])
        mine = blocks.at[k, :, y, core] if k % 2 == 0 else blocks.at[k, x, :, core]
        second = peer_y if k % 2 == 0 else peer_x
        for i in (1, 3, 2):
            send(mine, mine, plane_s, plane_r.at[k], second(i))

    def start_twin(k):
        if k == 0:
            recv(pieces.at[pl.ds(0, NCOL // 2 - 1)], line_r.at[0])
        else:
            recv(blocks.at[k, 0:3, :, 0], plane_r.at[k])
        mine = blocks.at[k, :, :, core]
        send(mine, mine, twin_s, twin_r.at[k], {"col": q + 1 - 2 * core})

    def ready(k):
        recv(blocks.at[k, :, :, 0], twin_r.at[k])

    def block_acts(k):
        return blocks[k].reshape(TOKENS // NZ, BLOCK)

    def over_tokens(a, b):
        return lax.dot_general(a, b, (((0,), (0,)), ((), ())), preferred_element_type=F32)

    def partial(s, offset):
        owner = lax.rem(z + offset + 2 * NZ, NZ)
        return fold(source[s, pl.ds(pl.multiple_of(owner * ROWS, 8), ROWS), :])

    def sum_kind(s):
        return max(0, s - 3)

    def sum_start(s):
        kind = sum_kind(s)
        across_out[s] = partial(s, NZ // 2).astype(BF16)
        for i, (rows, offset) in enumerate(halves):
            send(
                across_out.at[s, rows], across_in.at[s, rows], across_s.at[kind], across_r.at[s, i], at_z(offset)
            )
        for a in FAR_ORDER + (0,):
            for b in (1, 2):
                near_out[s, a, b - 1] = partial(s, FAR[a] + NEAR[b]).astype(BF16)
                send(
                    near_out.at[s, a, b - 1], near_in.at[s, a, b - 1],
                    near_s.at[kind], near_r.at[s, a], at_z(NEAR[b]),
                )

    def sum_middle(s):
        kind = sum_kind(s)
        for a in FAR_ORDER + (0,):
            total = partial(s, FAR[a])
            recv(near_in.at[s, a], near_r.at[s, a])
            for b in range(2):
                total = total + near_in[s, a, b].astype(F32)
            if a == 3:
                recv(across_in.at[s, 0:CUT], across_r.at[s, 0])
                top = total[:CUT] + across_in[s, 0:CUT].astype(F32)
                total = jnp.concatenate([top, total[CUT:]], axis=0)
            if a == 4:
                recv(across_in.at[s, CUT : CHUNK[0]], across_r.at[s, 1])
                low = total[CUT:] + across_in[s, CUT : CHUNK[0]].astype(F32)
                total = jnp.concatenate([total[:CUT], low], axis=0)
            if a:
                far_out[s, a - 1] = total.astype(BF16)
                send(far_out.at[s, a - 1], far_in.at[s, a - 1], far_s.at[kind], far_r.at[s], at_z(FAR[a]))
            else:
                near_sum[s] = total

    def sum_end(s):
        recv(far_in.at[s], far_r.at[s])
        total = near_sum[s]
        for a in range(4):
            total = total + far_in[s, a].astype(F32)
        return total

    def gradient(k):
        source[k] = over_tokens(block_acts(k), lowered[...])
        sum_start(k)

    def tile(k, t):
        lanes = pl.ds(pl.multiple_of(t * HALF, HALF), HALF)
        return blocks[k, :, :, :, :, lanes].reshape(TOKENS // NZ, HALF)

    def gram_first():
        for h in range(2):
            source[4, :, h * HALF : (h + 1) * HALF] = over_tokens(block_acts(1), tile(0, lax.rem(2 * (spot - GRAM_SPOT[0]) + h, TILES)))
        sum_start(4)

    def gram_rest():
        for h in range(2):
            item = lax.rem(2 * spot + h, 5 * TILES)
            pair = item // TILES
            later = (pair + 1) // 3
            source[5, :, h * HALF : (h + 1) * HALF] = over_tokens(
                block_acts(2 + later), tile(pair - 2 * later, lax.rem(item, TILES))
            )
        sum_start(5)

    def gram_send(kind):
        at = GRAM_AT[kind] + spot - GRAM_SPOT[kind]
        gram_in[at] = sum_end(4 + kind).astype(BF16)

        @pl.loop(1, NCOL)
        def _(i):
            send(gram_in.at[at], gram_in.at[at], gram_s.at[kind], gram_r.at[kind], at_col(i))

    def gram_recv(kind):
        count = GRAM_COUNT[kind]

        @pl.when(has_gram[kind])
        def _():
            recv(gram_in.at[pl.ds(0, count - 1)], gram_r.at[kind])

        @pl.when(jnp.logical_not(has_gram[kind]))
        def _():
            recv(gram_in.at[pl.ds(0, count)], gram_r.at[kind])

        for item in range((1, 5)[kind] * TILES):
            chunk = gram_in[GRAM_AT[kind] + item // 2].astype(F32)
            at = ROWS * (item % 2)
            lane = HALF * (item % TILES)
            gram[kind + item // TILES, :, lane : lane + HALF] = chunk[at : at + ROWS]

    def correction(k, j):
        return jnp.dot(gram[PAIR[k, j]].astype(BF16), delta[j], preferred_element_type=F32)

    scale = math.sqrt(CH)
    eta_unit = float(CH) / float(TOKENS)
    thresh_unit = math.sqrt(D)

    def shift(k, corrections):
        total = sum_end(k)
        whole = jnp.concatenate([total[:ROWS], total[ROWS:]], axis=1)
        for value in corrections:
            whole = whole + value / scale
        which = order_ref[k]
        current = weights_ref[which].astype(F32)
        for j in range(k):
            current = jnp.where(order_ref[j] == which, fresh_ref[j], current)
        shifted = current - (rate_ref[which] * eta_unit) * (whole / scale)
        square = shifted * shifted
        square = square[:, :HALF] + square[:, HALF:]
        square = jnp.concatenate([square, jnp.zeros((HALF - ROWS, HALF), F32)], axis=0)
        sums[k, q] = jnp.sum(square.T, axis=0, keepdims=True)

        @pl.loop(1, NCOL)
        def _(i):
            send(sums.at[k, q], sums.at[k, q], sum_s, sum_r.at[k], at_col(i))

        if k in EARLY:
            gather_start(k, shifted)
        return current, shifted

    def shrink(k, current, shifted, meanwhile=None):
        recv(sums.at[k, pl.ds(0, NCOL - 1)], sum_r.at[k])
        whole = jnp.sum(sums[k], axis=0)
        limit = penalty_ref[order_ref[k]] * thresh_unit
        factor = jnp.maximum(0.0, 1.0 - limit / jnp.sqrt(whole + 1e-06))
        row = factor
        factor = jnp.broadcast_to(row, (HALF, HALF)).T[:ROWS]
        fresh = jnp.concatenate([factor, factor], axis=1) * shifted
        fresh_ref[k] = fresh
        if k in EARLY:
            factors[k, z] = row

            @pl.loop(1, NZ)
            def _(i):
                send(factors.at[k, z], factors.at[k, z], factor_s, factor_r.at[k], at_z(i))

        else:
            gather_start(k, fresh - current)
        if meanwhile is not None:
            meanwhile()
        gather_forward(k)

    def collect(k):
        gather_collect(k)
        if k in EARLY:
            recv(factors.at[k, pl.ds(0, NZ - 1)], factor_r.at[k])
            table = jnp.concatenate([factors[k, j] for j in range(NZ)] + [jnp.zeros((HALF - NZ, HALF), F32)], axis=0).T
            for j in range(NZ):
                rows = slice(j * ROWS, (j + 1) * ROWS)
                change[rows, :] = change[rows, :] * table[:ROWS, j : j + 1]
            value = change[...] - held[k].astype(F32)
            for j in range(k):
                same = jnp.where(order_ref[j] == order_ref[k], 1.0, 0.0)
                value = value - same * delta[j].astype(F32)
            delta[k] = value.astype(BF16)
        else:
            delta[k] = change[...].astype(BF16)

    def update(k):
        out_ref[...] = out_ref[...] + (
            jnp.dot(block_acts(k), delta[k], preferred_element_type=F32) / scale
        )

    has_gram = [
        (spot >= GRAM_SPOT[kind]) & (spot < GRAM_SPOT[kind] + GRAM_COUNT[kind]) for kind in range(2)
    ]

    for k in EARLY:
        gather_forward(STEPS + EARLY.index(k))
    start_plane(1)
    start_twin(0)
    ready(0)
    gradient(0)
    start_plane(2)
    start_plane(3)
    start_twin(1)
    sum_middle(0)
    ready(1)
    pl.when(has_gram[0])(gram_first)
    gradient(1)
    start_twin(2)
    start_twin(3)

    for k in EARLY:
        gather_collect(STEPS + EARLY.index(k))
        held[k] = change[...].astype(BF16)

    current, shifted = shift(0, [])
    pl.when(has_gram[0])(lambda: sum_middle(4))
    sum_middle(1)
    shrink(0, current, shifted, lambda: pl.when(has_gram[0])(lambda: gram_send(0)))
    ready(2)
    ready(3)
    pl.when(has_gram[1])(gram_rest)
    gradient(2)
    collect(0)
    gram_recv(0)

    current, shifted = shift(1, [correction(1, 0)])
    update(0)
    pl.when(has_gram[1])(lambda: sum_middle(5))

    def beside():
        pl.when(has_gram[1])(lambda: gram_send(1))
        sum_middle(2)

    shrink(1, current, shifted, beside)
    gradient(3)
    collect(1)
    gram_recv(1)

    current, shifted = shift(2, [correction(2, 0), correction(2, 1)])
    update(1)
    early = [correction(3, 0), correction(3, 1)]
    sum_middle(3)
    shrink(2, current, shifted)
    collect(2)

    current, shifted = shift(3, early + [correction(3, 2)])
    update(2)
    shrink(3, current, shifted)
    collect(3)
    update(3)

    sent(pieces.at[pl.ds(0, NCOL - 1)], a2a_s)
    sent(pieces.at[pl.ds(0, NCOL // 2 - 1)], line_s.at[0])
    sent(blocks.at[1:STEPS, 0:3, 0, 0], line_s.at[1])
    sent(blocks.at[1:STEPS, 0:3, :, 0], plane_s)
    sent(blocks.at[:, :, :, 0], twin_s)
    sent(near_out.at[0:STEPS], near_s.at[0])
    sent(across_out.at[0:STEPS], across_s.at[0])
    sent(far_out.at[0:STEPS], far_s.at[0])
    sent(sums.at[:, pl.ds(0, NCOL - 1)], sum_s)
    sent(gathered.at[:, 1:5, 0], gf_s)
    sent(gathered.at[:, :, 1:3], gn_s)
    sent(opposite, go_s)
    sent(factors.at[0 : len(EARLY), pl.ds(0, NZ - 1)], factor_s)
    for kind in range(2):

        @pl.when(has_gram[kind])
        def _():
            sent(near_out.at[0], near_s.at[1 + kind])
            sent(across_out.at[0], across_s.at[1 + kind])
            sent(far_out.at[0], far_s.at[1 + kind])
            sent(gram_in.at[pl.ds(0, NCOL - 1)], gram_s.at[kind])


def place_kernel(order_ref, weights_ref, fresh_ref, out_ref):
    out_ref[...] = weights_ref[...].astype(F32)
    for k in range(STEPS):
        out_ref[order_ref[k]] = fresh_ref[k]


def body(acts, residual, weights, order, rate, penalty):
    smem = pl.BlockSpec(memory_space=pltpu.SMEM)
    vmem = pl.BlockSpec(memory_space=pltpu.VMEM)
    hbm = pl.BlockSpec(memory_space=pl.ANY)
    one = pltpu.SemaphoreType.DMA(())
    sems = pltpu.SemaphoreType.DMA
    fresh, resid = pl.pallas_call(
        kernel,
        out_shape=(
            jax.ShapeDtypeStruct((STEPS, ROWS, COLS), F32),
            jax.ShapeDtypeStruct(residual.shape, F32),
        ),
        in_specs=[hbm] * 6,
        out_specs=(vmem, vmem),
        scratch_shapes=[
            pltpu.SMEM((STEPS,), jnp.int32),
            pltpu.SMEM((NBLK,), F32),
            pltpu.SMEM((NBLK,), F32),
            pltpu.VMEM(weights.shape, BF16),
            pltpu.VMEM(residual.shape, BF16),
            pltpu.VMEM((NCOL, PIECE, BLOCK), BF16),
            pltpu.VMEM((STEPS, 4, 4, 2, PIECE, BLOCK), BF16),
            pltpu.VMEM((SETS, BLOCK, COLS), F32),
            pltpu.VMEM((SETS, 5, 2) + CHUNK, BF16),
            pltpu.VMEM((SETS, 5, 2) + CHUNK, BF16),
            pltpu.VMEM((SETS,) + CHUNK, BF16),
            pltpu.VMEM((SETS,) + CHUNK, BF16),
            pltpu.VMEM((SETS,) + CHUNK, F32),
            pltpu.VMEM((SETS, 4) + CHUNK, BF16),
            pltpu.VMEM((SETS, 4) + CHUNK, BF16),
            pltpu.VMEM((STEPS, NCOL, 1, HALF), F32),
            pltpu.VMEM((STEPS + len(EARLY), 5, 3) + CHUNK, BF16),
            pltpu.VMEM((STEPS + len(EARLY),) + CHUNK, BF16),
            pltpu.VMEM((BLOCK, COLS), F32),
            pltpu.VMEM((STEPS, BLOCK, COLS), BF16),
            pltpu.VMEM((STEPS, BLOCK, COLS), BF16),
            pltpu.VMEM((STEPS, NZ, 1, HALF), F32),
            pltpu.VMEM((NCOL,) + CHUNK, BF16),
            pltpu.VMEM((len(PAIR), ROWS, BLOCK), F32),
            sems((6,)),
            one, sems((STEPS,)), sems((STEPS,)), sems((STEPS,)), sems((SETS, 5)), sems((SETS, 2)),
            sems((SETS,)), sems((STEPS,)),
            sems((STEPS + len(EARLY), 4)), sems((STEPS + len(EARLY),)), sems((STEPS + len(EARLY),)), sems((2,)), sems((STEPS,)),
            one, sems((2,)), one, one, sems((3,)), sems((3,)), sems((3,)), one, one, one, one, sems((2,)), one,
        ],
        compiler_params=pltpu.CompilerParams(
            collective_id=0, has_side_effects=True, vmem_limit_bytes=62 * 1024 * 1024
        ),
        name="steps",
    )(order, rate, penalty, acts, residual, weights)
    pruned = pl.pallas_call(
        place_kernel,
        out_shape=jax.ShapeDtypeStruct(weights.shape, F32),
        in_specs=[smem, vmem, vmem],
        out_specs=vmem,
        compiler_params=pltpu.CompilerParams(vmem_limit_bytes=16 * 1024 * 1024),
        name="place",
    )(order, weights, fresh)
    return (pruned, resid)


def solution(mesh):
    in_specs = (P("tok", "col"), P("tok", "col"), P(None, "tok", "col"), P(), P(), P())
    out_specs = (P(None, "tok", "col"), P("tok", "col"))
    return jax.shard_map(body, mesh=mesh, in_specs=in_specs, out_specs=out_specs, check_vma=False)
```

```python
import math

import jax
import jax.numpy as jnp
from jax import lax
from jax.experimental import pallas as pl
from jax.experimental.pallas import tpu as pltpu
from jax.sharding import PartitionSpec as P

D = 8192
CH = 28672
STEPS = 4
NBLK = 32
BLOCK = 896
TOKENS = 8192
NZ = 16
NCOL = 32
ROWS = BLOCK // NZ
COLS = D // NCOL
PIECE = TOKENS // NZ // NCOL
HALF = COLS // 2
EARLY = (3,)
CHUNK = (2 * ROWS, HALF)
FAR = (0, 3, -3, 6, -6)
FAR_ORDER = (3, 4, 1, 2)
NEAR = (0, 1, -1)
CUT = 48
SETS = STEPS + 2
TILES = BLOCK // HALF
PAIR = {(1, 0): 0, (2, 0): 1, (2, 1): 2, (3, 0): 3, (3, 1): 4, (3, 2): 5}
GRAM_COUNT = ((TILES + 1) // 2, (5 * TILES + 1) // 2)
GRAM_AT = (0, GRAM_COUNT[0])
GRAM_SPOT = (GRAM_COUNT[1], 0)
MESH = pl.DeviceIdType.MESH
F32 = jnp.float32
BF16 = jnp.bfloat16


def fold(rows):
    return jnp.concatenate([rows[:, :HALF], rows[:, HALF:]], axis=0)


def unfold(chunk):
    wide = chunk.astype(F32)
    return jnp.concatenate([wide[:ROWS], wide[ROWS:]], axis=1)


def kernel(
    order_hbm, rate_hbm, penalty_hbm, acts_ref, resid_ref, weights_hbm,
    fresh_ref, out_ref,
    order_ref, rate_ref, penalty_ref, weights_ref, lowered,
    pieces, blocks, source, near_out, near_in, across_out, across_in, near_sum, far_out, far_in, sums, gathered, opposite, change, delta, held, factors,
    gram_in, gram,
    load_sems, a2a_r, line_r, plane_r, twin_r, near_r, across_r, far_r, sum_r, gf_r, gn_r, go_r, gram_r, factor_r,
    a2a_s, line_s, plane_s, twin_s, near_s, across_s, far_s, sum_s, gf_s, gn_s, go_s, gram_s, factor_s,
):
    z = lax.axis_index("tok")
    q = lax.axis_index("col")
    core = lax.rem(q, 2)
    y = lax.rem(q // 2, 4)
    x = q // 8
    spot = q // 2 + NCOL // 2 * core

    def at_z(offset):
        return {"tok": lax.rem(z + offset + 2 * NZ, NZ)}

    def at_col(i):
        return {"col": lax.rem(q + i, NCOL)}

    def for_columns(act):
        @pl.loop(0, NCOL - 1)
        def _(j):
            act(1 + lax.rem(j + NCOL // 2 - 1, NCOL - 1))

    def for_z(act):
        @pl.loop(0, NZ - 1)
        def _(j):
            act(NZ // 2 + ((j + 1) // 2) * (1 - 2 * lax.rem(j, 2)))

    def remote(src, dst, ssem, rsem, where):
        return pltpu.make_async_remote_copy(
            src_ref=src, dst_ref=dst, send_sem=ssem, recv_sem=rsem, device_id=where, device_id_type=MESH
        )

    def send(src, dst, ssem, rsem, where):
        remote(src, dst, ssem, rsem, where).start()

    def recv(ref, sem):
        remote(ref, ref, a2a_s, sem, at_z(1)).wait_recv()

    def sent(ref, sem):
        remote(ref, ref, sem, a2a_r, at_z(1)).wait_send()

    own_rows = pl.ds(pl.multiple_of(q * PIECE, PIECE), PIECE)
    loads = [
        pltpu.make_async_copy(src, dst, load_sems.at[i])
        for i, (src, dst) in enumerate((
            (acts_ref.at[own_rows], pieces.at[q]),
            (order_hbm, order_ref),
            (rate_hbm, rate_ref),
            (penalty_hbm, penalty_ref),
            (resid_ref, out_ref),
            (weights_hbm, weights_ref),
        ))
    ]
    for copy in loads:
        copy.start()

    barrier = pltpu.get_barrier_semaphore()

    for_z(lambda i: pl.semaphore_signal(barrier, inc=1, device_id=at_z(i), device_id_type=MESH))
    for_columns(lambda i: pl.semaphore_signal(barrier, inc=1, device_id=at_col(i), device_id_type=MESH))
    pl.semaphore_wait(barrier, NCOL - 1 + NZ - 1)

    halves = ((pl.ds(0, CUT), 2), (pl.ds(CUT, CHUNK[0] - CUT), -2))

    def gather_start(g, rows):
        gathered[g, 0, 0] = fold(rows).astype(BF16)
        for a in FAR_ORDER:
            send(gathered.at[g, 0, 0], gathered.at[g, a, 0], gf_s, gf_r.at[g, a - 1], at_z(FAR[a]))
        for b in (1, 2):
            send(gathered.at[g, 0, 0], gathered.at[g, 0, b], gn_s, gn_r.at[g], at_z(NEAR[b]))

    def gather_forward(g):
        for a in range(1, 5):
            recv(gathered.at[g, a, 0], gf_r.at[g, a - 1])
            if a >= 3:
                rows, offset = halves[a - 3]
                send(gathered.at[g, a, 0, rows], opposite.at[g, rows], go_s, go_r.at[g], at_z(offset))
            for b in (1, 2):
                send(gathered.at[g, a, 0], gathered.at[g, a, b], gn_s, gn_r.at[g], at_z(NEAR[b]))

    def gather_collect(g):
        def put(offset, chunk):
            owner = lax.rem(z - offset + 2 * NZ, NZ)
            change[pl.ds(pl.multiple_of(owner * ROWS, 8), ROWS), :] = unfold(chunk)

        for a in range(5):
            put(FAR[a], gathered[g, a, 0])
        recv(gathered.at[g, :, 1:3], gn_r.at[g])
        recv(opposite.at[g], go_r.at[g])
        for a in range(5):
            for b in (1, 2):
                put(FAR[a] + NEAR[b], gathered[g, a, b])
        put(NZ // 2, opposite[g])

    def send_piece(i):
        peer = lax.rem(q + i, NCOL)
        rows = pl.ds(pl.multiple_of(peer * PIECE, PIECE), PIECE)
        send(acts_ref.at[rows], pieces.at[q], a2a_s, a2a_r, at_col(i))

    for_columns(send_piece)

    for copy in loads:
        copy.wait()
    lowered[...] = out_ref[...].astype(BF16)
    for k in EARLY:
        gather_start(STEPS + EARLY.index(k), weights_ref[order_ref[k]].astype(F32))
    recv(pieces.at[pl.ds(0, NCOL - 1)], a2a_r)

    def peer_x(i):
        return {"col": (lax.rem(x + i, 4) * 4 + y) * 2 + core}

    def peer_y(i):
        return {"col": (x * 4 + lax.rem(y + i, 4)) * 2 + core}

    for k in range(STEPS):
        blocks[k, x, y, core] = pieces[order_ref[k]]
    first_piece = blocks.at[0, x, y, core]

    @pl.loop(0, NCOL // 2 - 1)
    def _(j):
        i = 1 + lax.rem(j + NCOL // 4 - 1, NCOL // 2 - 1)
        send(first_piece, first_piece, line_s.at[0], line_r.at[0], {"col": lax.rem(q + 2 * i, NCOL)})

    for k in range(1, STEPS):
        mine = blocks.at[k, x, y, core]
        first = peer_x if k % 2 == 0 else peer_y
        for i in (1, 3, 2):
            send(mine, mine, line_s.at[1], line_r.at[k], first(i))

    def start_plane(k):
        recv(blocks.at[k, 0:3, 0, 0], line_r.at[k])
        mine = blocks.at[k, :, y, core] if k % 2 == 0 else blocks.at[k, x, :, core]
        second = peer_y if k % 2 == 0 else peer_x
        for i in (1, 3, 2):
            send(mine, mine, plane_s, plane_r.at[k], second(i))

    def start_twin(k):
        if k == 0:
            recv(pieces.at[pl.ds(0, NCOL // 2 - 1)], line_r.at[0])
        else:
            recv(blocks.at[k, 0:3, :, 0], plane_r.at[k])
        mine = blocks.at[k, :, :, core]
        send(mine, mine, twin_s, twin_r.at[k], {"col": q + 1 - 2 * core})

    def ready(k):
        recv(blocks.at[k, :, :, 0], twin_r.at[k])

    def block_acts(k):
        return blocks[k].reshape(TOKENS // NZ, BLOCK)

    def over_tokens(a, b):
        return lax.dot_general(a, b, (((0,), (0,)), ((), ())), preferred_element_type=F32)

    def partial(s, offset):
        owner = lax.rem(z + offset + 2 * NZ, NZ)
        return fold(source[s, pl.ds(pl.multiple_of(owner * ROWS, 8), ROWS), :])

    def sum_kind(s):
        return max(0, s - 3)

    def sum_start(s):
        kind = sum_kind(s)
        across_out[s] = partial(s, NZ // 2).astype(BF16)
        for i, (rows, offset) in enumerate(halves):
            send(
                across_out.at[s, rows], across_in.at[s, rows], across_s.at[kind], across_r.at[s, i], at_z(offset)
            )
        for a in FAR_ORDER + (0,):
            for b in (1, 2):
                near_out[s, a, b - 1] = partial(s, FAR[a] + NEAR[b]).astype(BF16)
                send(
                    near_out.at[s, a, b - 1], near_in.at[s, a, b - 1],
                    near_s.at[kind], near_r.at[s, a], at_z(NEAR[b]),
                )

    def sum_middle(s):
        kind = sum_kind(s)
        for a in FAR_ORDER + (0,):
            total = partial(s, FAR[a])
            recv(near_in.at[s, a], near_r.at[s, a])
            for b in range(2):
                total = total + near_in[s, a, b].astype(F32)
            if a == 3:
                recv(across_in.at[s, 0:CUT], across_r.at[s, 0])
                top = total[:CUT] + across_in[s, 0:CUT].astype(F32)
                total = jnp.concatenate([top, total[CUT:]], axis=0)
            if a == 4:
                recv(across_in.at[s, CUT : CHUNK[0]], across_r.at[s, 1])
                low = total[CUT:] + across_in[s, CUT : CHUNK[0]].astype(F32)
                total = jnp.concatenate([total[:CUT], low], axis=0)
            if a:
                far_out[s, a - 1] = total.astype(BF16)
                send(far_out.at[s, a - 1], far_in.at[s, a - 1], far_s.at[kind], far_r.at[s], at_z(FAR[a]))
            else:
                near_sum[s] = total

    def sum_end(s):
        recv(far_in.at[s], far_r.at[s])
        total = near_sum[s]
        for a in range(4):
            total = total + far_in[s, a].astype(F32)
        return total

    def gradient(k):
        source[k] = over_tokens(block_acts(k), lowered[...])
        sum_start(k)

    def tile(k, t):
        lanes = pl.ds(pl.multiple_of(t * HALF, HALF), HALF)
        return blocks[k, :, :, :, :, lanes].reshape(TOKENS // NZ, HALF)

    def gram_first():
        for h in range(2):
            source[4, :, h * HALF : (h + 1) * HALF] = over_tokens(block_acts(1), tile(0, lax.rem(2 * (spot - GRAM_SPOT[0]) + h, TILES)))
        sum_start(4)

    def gram_rest():
        for h in range(2):
            item = lax.rem(2 * spot + h, 5 * TILES)
            pair = item // TILES
            later = (pair + 1) // 3
            source[5, :, h * HALF : (h + 1) * HALF] = over_tokens(
                block_acts(2 + later), tile(pair - 2 * later, lax.rem(item, TILES))
            )
        sum_start(5)

    def gram_send(kind):
        at = GRAM_AT[kind] + spot - GRAM_SPOT[kind]
        gram_in[at] = sum_end(4 + kind).astype(BF16)

        for_columns(
            lambda i: send(gram_in.at[at], gram_in.at[at], gram_s.at[kind], gram_r.at[kind], at_col(i))
        )

    def gram_recv(kind):
        count = GRAM_COUNT[kind]

        @pl.when(has_gram[kind])
        def _():
            recv(gram_in.at[pl.ds(0, count - 1)], gram_r.at[kind])

        @pl.when(jnp.logical_not(has_gram[kind]))
        def _():
            recv(gram_in.at[pl.ds(0, count)], gram_r.at[kind])

        for item in range((1, 5)[kind] * TILES):
            chunk = gram_in[GRAM_AT[kind] + item // 2].astype(F32)
            at = ROWS * (item % 2)
            lane = HALF * (item % TILES)
            gram[kind + item // TILES, :, lane : lane + HALF] = chunk[at : at + ROWS]

    def correction(k, j):
        return jnp.dot(gram[PAIR[k, j]].astype(BF16), delta[j], preferred_element_type=F32)

    scale = math.sqrt(CH)
    eta_unit = float(CH) / float(TOKENS)
    thresh_unit = math.sqrt(D)

    def shift(k, corrections):
        total = sum_end(k)
        whole = jnp.concatenate([total[:ROWS], total[ROWS:]], axis=1)
        for value in corrections:
            whole = whole + value / scale
        which = order_ref[k]
        current = weights_ref[which].astype(F32)
        for j in range(k):
            current = jnp.where(order_ref[j] == which, fresh_ref[j], current)
        shifted = current - (rate_ref[which] * eta_unit) * (whole / scale)
        square = shifted * shifted
        square = square[:, :HALF] + square[:, HALF:]
        square = jnp.concatenate([square, jnp.zeros((HALF - ROWS, HALF), F32)], axis=0)
        sums[k, q] = jnp.sum(square.T, axis=0, keepdims=True)

        for_columns(lambda i: send(sums.at[k, q], sums.at[k, q], sum_s, sum_r.at[k], at_col(i)))

        if k in EARLY:
            gather_start(k, shifted)
        return current, shifted

    def shrink(k, current, shifted, meanwhile=None):
        recv(sums.at[k, pl.ds(0, NCOL - 1)], sum_r.at[k])
        whole = jnp.sum(sums[k], axis=0)
        limit = penalty_ref[order_ref[k]] * thresh_unit
        factor = jnp.maximum(0.0, 1.0 - limit / jnp.sqrt(whole + 1e-06))
        row = factor
        factor = jnp.broadcast_to(row, (HALF, HALF)).T[:ROWS]
        fresh = jnp.concatenate([factor, factor], axis=1) * shifted
        fresh_ref[k] = fresh
        if k in EARLY:
            factors[k, z] = row

            for_z(lambda i: send(factors.at[k, z], factors.at[k, z], factor_s, factor_r.at[k], at_z(i)))

        else:
            gather_start(k, fresh - current)
        if meanwhile is not None:
            meanwhile()
        gather_forward(k)

    def collect(k):
        gather_collect(k)
        if k in EARLY:
            recv(factors.at[k, pl.ds(0, NZ - 1)], factor_r.at[k])
            table = jnp.concatenate([factors[k, j] for j in range(NZ)] + [jnp.zeros((HALF - NZ, HALF), F32)], axis=0).T
            for j in range(NZ):
                rows = slice(j * ROWS, (j + 1) * ROWS)
                change[rows, :] = change[rows, :] * table[:ROWS, j : j + 1]
            value = change[...] - held[k].astype(F32)
            for j in range(k):
                same = jnp.where(order_ref[j] == order_ref[k], 1.0, 0.0)
                value = value - same * delta[j].astype(F32)
            delta[k] = value.astype(BF16)
        else:
            delta[k] = change[...].astype(BF16)

    def update(k):
        out_ref[...] = out_ref[...] + (
            jnp.dot(block_acts(k), delta[k], preferred_element_type=F32) / scale
        )

    has_gram = [
        (spot >= GRAM_SPOT[kind]) & (spot < GRAM_SPOT[kind] + GRAM_COUNT[kind]) for kind in range(2)
    ]

    for k in EARLY:
        gather_forward(STEPS + EARLY.index(k))
    start_plane(1)
    start_twin(0)
    ready(0)
    gradient(0)
    start_plane(2)
    start_plane(3)
    start_twin(1)
    sum_middle(0)
    ready(1)
    pl.when(has_gram[0])(gram_first)
    gradient(1)
    start_twin(2)
    start_twin(3)

    for k in EARLY:
        gather_collect(STEPS + EARLY.index(k))
        held[k] = change[...].astype(BF16)

    current, shifted = shift(0, [])
    pl.when(has_gram[0])(lambda: sum_middle(4))
    sum_middle(1)
    shrink(0, current, shifted, lambda: pl.when(has_gram[0])(lambda: gram_send(0)))
    ready(2)
    ready(3)
    pl.when(has_gram[1])(gram_rest)
    gradient(2)
    collect(0)
    gram_recv(0)

    current, shifted = shift(1, [correction(1, 0)])
    update(0)
    pl.when(has_gram[1])(lambda: sum_middle(5))

    def beside():
        pl.when(has_gram[1])(lambda: gram_send(1))
        sum_middle(2)

    shrink(1, current, shifted, beside)
    gradient(3)
    collect(1)
    gram_recv(1)

    current, shifted = shift(2, [correction(2, 0), correction(2, 1)])
    update(1)
    early = [correction(3, 0), correction(3, 1)]
    sum_middle(3)
    shrink(2, current, shifted)
    collect(2)

    current, shifted = shift(3, early + [correction(3, 2)])
    update(2)
    shrink(3, current, shifted)
    collect(3)
    update(3)

    sent(pieces.at[pl.ds(0, NCOL - 1)], a2a_s)
    sent(pieces.at[pl.ds(0, NCOL // 2 - 1)], line_s.at[0])
    sent(blocks.at[1:STEPS, 0:3, 0, 0], line_s.at[1])
    sent(blocks.at[1:STEPS, 0:3, :, 0], plane_s)
    sent(blocks.at[:, :, :, 0], twin_s)
    sent(near_out.at[0:STEPS], near_s.at[0])
    sent(across_out.at[0:STEPS], across_s.at[0])
    sent(far_out.at[0:STEPS], far_s.at[0])
    sent(sums.at[:, pl.ds(0, NCOL - 1)], sum_s)
    sent(gathered.at[:, 1:5, 0], gf_s)
    sent(gathered.at[:, :, 1:3], gn_s)
    sent(opposite, go_s)
    sent(factors.at[0 : len(EARLY), pl.ds(0, NZ - 1)], factor_s)
    for kind in range(2):

        @pl.when(has_gram[kind])
        def _():
            sent(near_out.at[0], near_s.at[1 + kind])
            sent(across_out.at[0], across_s.at[1 + kind])
            sent(far_out.at[0], far_s.at[1 + kind])
            sent(gram_in.at[pl.ds(0, NCOL - 1)], gram_s.at[kind])


def place_kernel(order_ref, weights_ref, fresh_ref, out_ref):
    out_ref[...] = weights_ref[...].astype(F32)
    for k in range(STEPS):
        out_ref[order_ref[k]] = fresh_ref[k]


def body(acts, residual, weights, order, rate, penalty):
    smem = pl.BlockSpec(memory_space=pltpu.SMEM)
    vmem = pl.BlockSpec(memory_space=pltpu.VMEM)
    hbm = pl.BlockSpec(memory_space=pl.ANY)
    one = pltpu.SemaphoreType.DMA(())
    sems = pltpu.SemaphoreType.DMA
    fresh, resid = pl.pallas_call(
        kernel,
        out_shape=(
            jax.ShapeDtypeStruct((STEPS, ROWS, COLS), F32),
            jax.ShapeDtypeStruct(residual.shape, F32),
        ),
        in_specs=[hbm] * 6,
        out_specs=(vmem, vmem),
        scratch_shapes=[
            pltpu.SMEM((STEPS,), jnp.int32),
            pltpu.SMEM((NBLK,), F32),
            pltpu.SMEM((NBLK,), F32),
            pltpu.VMEM(weights.shape, BF16),
            pltpu.VMEM(residual.shape, BF16),
            pltpu.VMEM((NCOL, PIECE, BLOCK), BF16),
            pltpu.VMEM((STEPS, 4, 4, 2, PIECE, BLOCK), BF16),
            pltpu.VMEM((SETS, BLOCK, COLS), F32),
            pltpu.VMEM((SETS, 5, 2) + CHUNK, BF16),
            pltpu.VMEM((SETS, 5, 2) + CHUNK, BF16),
            pltpu.VMEM((SETS,) + CHUNK, BF16),
            pltpu.VMEM((SETS,) + CHUNK, BF16),
            pltpu.VMEM((SETS,) + CHUNK, F32),
            pltpu.VMEM((SETS, 4) + CHUNK, BF16),
            pltpu.VMEM((SETS, 4) + CHUNK, BF16),
            pltpu.VMEM((STEPS, NCOL, 1, HALF), F32),
            pltpu.VMEM((STEPS + len(EARLY), 5, 3) + CHUNK, BF16),
            pltpu.VMEM((STEPS + len(EARLY),) + CHUNK, BF16),
            pltpu.VMEM((BLOCK, COLS), F32),
            pltpu.VMEM((STEPS, BLOCK, COLS), BF16),
            pltpu.VMEM((STEPS, BLOCK, COLS), BF16),
            pltpu.VMEM((STEPS, NZ, 1, HALF), F32),
            pltpu.VMEM((NCOL,) + CHUNK, BF16),
            pltpu.VMEM((len(PAIR), ROWS, BLOCK), F32),
            sems((6,)),
            one, sems((STEPS,)), sems((STEPS,)), sems((STEPS,)), sems((SETS, 5)), sems((SETS, 2)),
            sems((SETS,)), sems((STEPS,)),
            sems((STEPS + len(EARLY), 4)), sems((STEPS + len(EARLY),)), sems((STEPS + len(EARLY),)), sems((2,)), sems((STEPS,)),
            one, sems((2,)), one, one, sems((3,)), sems((3,)), sems((3,)), one, one, one, one, sems((2,)), one,
        ],
        compiler_params=pltpu.CompilerParams(
            collective_id=0, has_side_effects=True, vmem_limit_bytes=62 * 1024 * 1024
        ),
        name="steps",
    )(order, rate, penalty, acts, residual, weights)
    pruned = pl.pallas_call(
        place_kernel,
        out_shape=jax.ShapeDtypeStruct(weights.shape, F32),
        in_specs=[smem, vmem, vmem],
        out_specs=vmem,
        compiler_params=pltpu.CompilerParams(vmem_limit_bytes=16 * 1024 * 1024),
        name="place",
    )(order, weights, fresh)
    return (pruned, resid)


def solution(mesh):
    in_specs = (P("tok", "col"), P("tok", "col"), P(None, "tok", "col"), P(), P(), P())
    out_specs = (P(None, "tok", "col"), P("tok", "col"))
    return jax.shard_map(body, mesh=mesh, in_specs=in_specs, out_specs=out_specs, check_vma=False)
```
